512 devices in a mesh: ctx: 16 (over x, z_hi, core), exp: 32 (over y, z_lo).
Axes of the slice: x: 4, y: 4, z: 16 (z_hi: 2, z_lo: 8; z = z_hi * 8 + z_lo), core: 2. Of those that a mesh axis runs over, the one named last changes fastest.
Arguments:
- queries: bfloat16 [32, 2048, 2048], P('exp', 'ctx'), may hold values from -6 to 6
- keys: bfloat16 [32, 2048, 256], P('exp', 'ctx'), may hold values from -6 to 6
- values: bfloat16 [32, 2048, 256], P('exp', 'ctx'), may hold values from -6 to 6
- segments: int32 [32, 2048], P('exp', 'ctx'), may hold values from 0 to 7, never falling along the last dimension, each value on 1 to 1024 neighbouring positions
- residual: bfloat16 [32, 2048, 2048], P('exp', 'ctx'), may hold values from -6 to 6
- norm_gain: bfloat16 [2048], replicated, may hold values from 0.25 to 1.75
- expert_ids: int32 [32, 2048, 8], P('exp', 'ctx'), may hold values from 0 to 31, all different within a row; in each aligned block of 128 rows (0 to 127, 128 to 255, ..., all dimensions but the last counted through in order) at most 36 rows name the same one
- gate_weights: float32 [32, 2048, 8], P('exp', 'ctx'), may hold values from 0.1 to 1
- w_gate: bfloat16 [32, 2048, 384], P('exp', 'ctx'), may hold values from -0.125 to 0.125
- w_up: bfloat16 [32, 2048, 384], P('exp', 'ctx'), may hold values from -0.125 to 0.125
- w_down: bfloat16 [32, 384, 2048], P('exp', None, 'ctx'), may hold values from -0.3125 to 0.3125
Outputs:
- layer_out: bfloat16 [32, 2048, 2048], P('exp', 'ctx')
The draws below stay inside these ranges and needn't reach their ends.
Inputs may be any that keep to these rules, and one draw needn't show every extreme that they name: `expert_ids`: each row names 8 different experts. Among the rows of one device (aligned blocks of 128 rows) no expert is named more than 36 times, and some device reaches 36. `segments`: within a sequence the ids never fall; each document has 1 to 1024 positions and one has exactly 1024.
All inputs are finite; a program needn't handle non-finite values.
Results may differ from the reference program's by a relative error of at most 0.0085.
Values may be sent and summed in bfloat16 or wider, within the bound.
No kernel may reach another device: no remote copies, remote signals or barrier semaphores. Data moves between devices by JAX's collectives and lax.ppermute only.
A program may use at most 64 MiB of HBM per device.

```python
import math
import jax
import jax.numpy as jnp
import numpy as np
from jax import lax

D = 2048
HEADS = 16
KVH = 2
HD = 128
FF = 384
EXPERTS = 32
TOPK = 8
DOCS = 8
TOK = 128
CAP = 36
LENGTH = 2048
SEQS = 32
N_CTX = 16
N_EXP = 32


def draw_queries(key, part):
    key = jax.random.fold_in(key, 11)
    base = jnp.clip(jax.random.normal(key, (SEQS, LENGTH, HEADS * HD), jnp.float32), -6.0, 6.0)
    return base.astype(jnp.bfloat16)


def draw_keys(key, part):
    key = jax.random.fold_in(key, 23)
    base = jnp.clip(jax.random.normal(key, (SEQS, LENGTH, KVH * HD), jnp.float32), -6.0, 6.0)
    return base.astype(jnp.bfloat16)


def block_levels(key, shape, shards, smallest, top_value):
    def one(axis_at, blocks):
        heights = jax.random.uniform(jax.random.fold_in(jax.random.fold_in(key, 6), axis_at), (blocks,), jnp.float32, smallest / len(shards), top_value / len(shards))
        return jnp.repeat(jnp.exp(heights), shape[axis_at] // blocks).reshape((-1,) + (1,) * (len(shape) - axis_at - 1))

    loudness = one(*shards[0])
    for cut in shards[1:]:
        loudness = loudness * one(*cut)
    return loudness


def profile(number_of, total, most, slope):
    weights = [(1 << 20) // math.isqrt(standing ** slope) + 1 for standing in range(2, number_of + 1)]
    rest, holding = total - most - (number_of - 1), [1] * (number_of - 1)
    while rest > 0:
        candidates = [i for i in range(number_of - 1) if holding[i] < most]
        mass, remaining = sum([weights[i] for i in candidates]), rest
        for i in candidates:
            addition = min(most - holding[i], max(1, remaining * weights[i] // mass), rest)
            holding[i] = holding[i] + addition
            rest = rest - addition
    return np.array([most] + holding)


def uneven_parts(stream_key, amount, total, limit, slope):
    if amount == 2:
        one = jax.random.randint(stream_key, (), max(1, total - limit), min(limit, total - 1) + 1)
        return jnp.stack([one, total - one])
    lengths = jnp.asarray(profile(amount, total, limit, slope), jnp.int32)
    pairs = (amount - 1) // 2
    source_of, taker = lengths[1:1 + 2 * pairs:2], lengths[2:2 + 2 * pairs:2]
    room = jnp.minimum(source_of - 1, limit - taker)
    shifted = jax.random.randint(jax.random.fold_in(stream_key, 1), (pairs,), 0, 1 << 20) % (room + 1)
    lengths = lengths.at[1:1 + 2 * pairs:2].set(source_of - shifted).at[2:2 + 2 * pairs:2].set(taker + shifted)
    return lengths[jax.random.permutation(jax.random.fold_in(stream_key, 2), amount)]


def deal_out(rng, own, number, rows, count, top, most, skew):
    sequence = jax.random.permutation(rng, count)
    crowded, ordinary = portions_of(count, rows * top, most, skew, True), portions_of(count, rows * top, most, skew, False)
    places = jnp.arange(count)

    def named(lengths, offset_by):
        used = int((lengths > 0).sum())
        fixed = max(1, used // 4)
        shifted = fixed + (places - fixed + offset_by * (used - fixed)) % max(1, count - fixed)
        return jnp.zeros((count,), jnp.int32).at[sequence[jnp.where(places < fixed, places, shifted)]].set(jnp.asarray(lengths, jnp.int32))

    lengths = jnp.where(number % 4 == 0, named(crowded, number // 4), named(ordinary, number - number // 4 - 1))
    mixed = jax.random.permutation(jax.random.fold_in(own, 3), count)
    donor, receiver = mixed[0:count // 2 * 2:2], mixed[1:count // 2 * 2:2]
    room = jnp.minimum(lengths[donor] - 1, most - lengths[receiver]) // 2
    room = jnp.where((donor == sequence[0]) | (receiver == sequence[0]) | (lengths[receiver] == 0), 0, jnp.maximum(room, 0))
    shifted = jax.random.randint(jax.random.fold_in(own, 4), (count // 2,), 0, 1 << 20) % (room + 1)
    lengths = lengths.at[donor].add(-shifted).at[receiver].add(shifted)
    items = jnp.searchsorted(jnp.cumsum(lengths), jnp.arange(rows * top), side="right").astype(jnp.int32)
    table = items.reshape(top, rows).T
    table = table[jax.random.permutation(jax.random.fold_in(own, 1), rows)]
    offset_by = jax.random.randint(jax.random.fold_in(own, 2), (rows, 1), 0, top)
    return jnp.take_along_axis(table, (jnp.arange(top)[None, :] + offset_by) % top, axis=1)


def portions_of(amount, total, reach, skew, full):
    portions = [(1 << 20) // math.isqrt(rank ** skew) + 1 for rank in range(1, amount + 1)]
    largest = reach if full else min(reach, max(-(-total // amount), total * portions[0] // sum(portions)))
    least = 1 if total - largest >= amount - 1 else 0
    holding, rest = [largest] + [least] * (amount - 1), total - largest - least * (amount - 1)
    while rest > 0:
        candidates = [i for i in range(1, amount) if holding[i] < largest] or [i for i in range(1, amount) if holding[i] < reach]
        pool, left = sum([portions[i] for i in candidates]), rest
        for i in candidates:
            extra = min(reach - holding[i], max(1, left * portions[i] // pool), rest)
            holding[i] = holding[i] + extra
            rest = rest - extra
    return np.array(holding)


def noise(stream_key, extent, deviation, most, cuts=(), kind=jnp.bfloat16):
    array = jax.random.normal(stream_key, extent, jnp.float32) * deviation
    if len(cuts) > 0:
        array = block_levels(stream_key, extent, cuts, -0.22, 0.18) * array
    return jnp.clip(array, min=-most, max=most).astype(kind)


def setup_inputs(seed: int = 0) -> dict:
    seeds = jax.random.split(jax.random.key(seed), 12)
    queries = draw_queries(jax.random.fold_in(seeds[11], 71), 0)
    keys = draw_keys(jax.random.fold_in(seeds[11], 71), 0)
    values = noise(seeds[2], (SEQS, LENGTH, KVH * HD), 1.0, 6.0, ((0, 32), (1, 16)))
    segments = jax.vmap(lambda own: jnp.searchsorted(jnp.cumsum(uneven_parts(own, DOCS, LENGTH, LENGTH // 2, 1)), jnp.arange(LENGTH), side="right"))(jax.random.split(seeds[3], SEQS)).reshape((SEQS, LENGTH)).astype(jnp.int32)
    residual = noise(seeds[4], (SEQS, LENGTH, D), 1.0, 6.0, ((0, 32), (1, 16)))
    norm_gain = jnp.clip(1.0 + 0.15 * jax.random.normal(seeds[5], (D,), jnp.float32), 0.25, 1.75).astype(jnp.bfloat16)
    expert_ids_keys = jax.random.split(jax.random.fold_in(seeds[6], 1), SEQS * LENGTH // TOK)
    expert_ids_turns = jax.random.permutation(jax.random.fold_in(seeds[6], 3), SEQS * LENGTH // TOK)
    expert_ids = jax.vmap(lambda own, number: deal_out(jax.random.fold_in(seeds[6], 2), own, number, TOK, EXPERTS, TOPK, CAP, 1))(expert_ids_keys, expert_ids_turns).reshape((SEQS, LENGTH, TOPK))
    gate_weights = jnp.clip(jnp.exp(math.log(1.0) - 2.3025851 * jax.random.uniform(seeds[7], (SEQS, LENGTH, TOPK), jnp.float32) ** block_levels(seeds[7], (SEQS, LENGTH, TOPK), ((0, 32), (1, 16)), -0.2, 0.2)), 0.1, 1.0)
    w_gate = noise(seeds[8], (EXPERTS, D, FF), D ** -0.5, 0.125, ((0, 32), (1, 16)))
    w_up = noise(seeds[9], (EXPERTS, D, FF), D ** -0.5, 0.125, ((0, 32), (1, 16)))
    w_down = noise(seeds[10], (EXPERTS, FF, D), FF ** -0.5, 0.3125, ((0, 32), (2, 16)))
    return {"queries": queries, "keys": keys, "values": values, "segments": segments, "residual": residual, "norm_gain": norm_gain, "expert_ids": expert_ids, "gate_weights": gate_weights, "w_gate": w_gate, "w_up": w_up, "w_down": w_down}


def attend_sequence(operands):
    queries, keys, values, segments = operands
    length = queries.shape[0]
    groups = HEADS // KVH
    query_f = queries.astype(jnp.float32).reshape(length, KVH, groups, HD)
    key_f = keys.astype(jnp.float32).reshape(length, KVH, HD)
    value_f = values.astype(jnp.float32).reshape(length, KVH, HD)
    scores = jnp.einsum('tgjd,sgd->gjts', query_f, key_f, precision=lax.Precision.HIGHEST) * HD ** (-0.5)
    positions = jnp.arange(length, dtype=jnp.int32)
    allowed = (segments[:, None] == segments[None, :]) & (positions[None, :] <= positions[:, None])
    scores = jnp.where(allowed, scores, -1e+30)
    peak_score = lax.optimization_barrier(jnp.max(scores, axis=-1, keepdims=True))
    weights = jnp.where(allowed, jnp.exp(scores - peak_score), 0.0)
    denominator = lax.optimization_barrier(jnp.sum(weights, axis=-1))
    rounded = lax.optimization_barrier(weights.astype(jnp.bfloat16)).astype(jnp.float32)
    attended = jnp.einsum('gjts,sgd->gjtd', rounded, value_f, precision=lax.Precision.HIGHEST) / denominator[..., None]
    return jnp.transpose(attended, (2, 0, 1, 3)).reshape(length, HEADS * HD)

def reference(queries, keys, values, segments, residual, norm_gain, expert_ids, gate_weights, w_gate, w_up, w_down):
    attended = lax.map(attend_sequence, (queries, keys, values, segments))
    hidden_state = (residual.astype(jnp.float32) + attended).reshape(-1, D)
    normed = (hidden_state * lax.rsqrt(lax.optimization_barrier(jnp.mean(hidden_state * hidden_state, axis=-1, keepdims=True)) + 1e-06) * norm_gain.astype(jnp.float32)).astype(jnp.bfloat16)
    row_count = hidden_state.shape[0]
    flat_ids = expert_ids.reshape(-1).astype(jnp.int32)
    flat_gates = gate_weights.reshape(-1)
    owners = (jnp.arange(row_count * TOPK, dtype=jnp.int32) // TOPK).astype(jnp.int32)
    sorted_pairs = jnp.argsort(flat_ids, stable=True).astype(jnp.int32)
    per_expert = lax.optimization_barrier(jnp.sum((flat_ids[None, :] == jnp.arange(EXPERTS, dtype=jnp.int32)[:, None]).astype(jnp.int32), axis=1)).astype(jnp.int32)
    first_slot = (jnp.cumsum(per_expert) - per_expert).astype(jnp.int32)
    slot_limit = N_CTX * N_EXP * CAP
    padded = jnp.concatenate([sorted_pairs, jnp.zeros((slot_limit,), jnp.int32)])

    def one_expert(expert, routed):
        picked = lax.dynamic_slice_in_dim(padded, first_slot[expert], slot_limit)
        live_slot = jnp.arange(slot_limit, dtype=jnp.int32) < per_expert[expert]
        tokens_in = normed[owners[picked]]
        gate_value = jnp.dot(tokens_in, w_gate[expert], preferred_element_type=jnp.float32)
        upward = jnp.dot(tokens_in, w_up[expert], preferred_element_type=jnp.float32)
        inner_act = (jax.nn.silu(gate_value) * upward).astype(jnp.bfloat16)
        expert_out = jnp.dot(inner_act, w_down[expert], preferred_element_type=jnp.float32).astype(jnp.bfloat16)
        factor = jnp.where(live_slot, flat_gates[picked], 0.0)
        return routed.at[owners[picked]].add(expert_out.astype(jnp.float32) * factor[:, None])
    routed = lax.fori_loop(0, EXPERTS, one_expert, jnp.zeros((row_count, D), jnp.float32))
    return (hidden_state + routed).astype(jnp.bfloat16).reshape(residual.shape)
```

```python
import functools

import jax
import jax.numpy as jnp
from jax import lax
from jax.experimental import pallas as pl
from jax.experimental.pallas import tpu as pltpu
from jax.sharding import Mesh, PartitionSpec as P

D = 2048
HEADS = 16
KVH = 2
GROUPS = HEADS // KVH
HD = 128
FF = 384
EXPERTS = 32
TOPK = 8
TOK = 128
CAP = 36
SLOTS = EXPERTS * CAP
PACK = 144
WINDOW = 9
BLOCKS = 12
AXES = ("x", "zh", "c", "y", "zl")
F32 = jnp.float32
BF16 = jnp.bfloat16
NT = (((1,), (1,)), ((), ()))


def params(mib):
    return pltpu.CompilerParams(vmem_limit_bytes=mib * 1024 * 1024)


def slot_kernel(ids_ref, gates_ref, send_ref, high_ref, low_ref):
    ids = ids_ref[...]
    gates = gates_ref[...]
    column = lax.broadcasted_iota(jnp.int32, (TOK, EXPERTS), 1)
    named = jnp.zeros((TOK, EXPERTS), F32)
    gate = jnp.zeros((TOK, EXPERTS), F32)
    for k in range(TOPK):
        hit = ids[:, k : k + 1] == column
        named = named + jnp.where(hit, 1.0, 0.0)
        gate = gate + jnp.where(hit, gates[:, k : k + 1], 0.0)
    row = lax.broadcasted_iota(jnp.int32, (TOK, TOK), 0)
    earlier = (lax.broadcasted_iota(jnp.int32, (TOK, TOK), 1) < row).astype(F32).astype(BF16)
    rank = jnp.dot(earlier, named.astype(BF16), preferred_element_type=F32)
    rank = jnp.where(named > 0.0, rank, -1.0).astype(BF16)
    slot = lax.broadcasted_iota(jnp.int32, (SLOTS, EXPERTS), 0).astype(F32)
    owner = jnp.floor((slot + 0.5) * (1.0 / CAP))
    place = slot - CAP * owner
    expert = lax.broadcasted_iota(jnp.int32, (SLOTS, EXPERTS), 1).astype(F32)
    spread = jnp.where(owner == expert, 1.0, 0.0).astype(BF16)
    rank_rows = lax.dot_general(spread, rank, NT, preferred_element_type=F32)
    send_ref[...] = jnp.where(rank_rows == place[:, :1], 1.0, 0.0).astype(BF16)
    slot_t = lax.broadcasted_iota(jnp.int32, (1, SLOTS), 1).astype(F32)
    place_t = slot_t - CAP * jnp.floor((slot_t + 0.5) * (1.0 / CAP))
    taken = lax.dot_general(rank, spread, NT, preferred_element_type=F32) == place_t
    high = gate.astype(BF16)
    low = (gate - high.astype(F32)).astype(BF16)
    for part, ref in ((high, high_ref), (low, low_ref)):
        wide = lax.dot_general(part, spread, NT, preferred_element_type=F32)
        ref[...] = jnp.where(taken, wide, 0.0).astype(BF16)


def slot_matrices(ids, gates):
    return pl.pallas_call(
        slot_kernel,
        out_shape=(
            jax.ShapeDtypeStruct((SLOTS, TOK), BF16),
            jax.ShapeDtypeStruct((TOK, SLOTS), BF16),
            jax.ShapeDtypeStruct((TOK, SLOTS), BF16),
        ),
        compiler_params=params(32),
        cost_estimate=pl.CostEstimate(flops=40_000_000, bytes_accessed=1_000_000, transcendentals=0),
        name="slots",
    )(ids, gates)


def attention_kernel(where_ref, q_hbm, seg_ref, res_hbm, gain_ref, send_ref, *rest):
    blocks = rest[:BLOCKS]
    hidden_ref, out_ref, kv, segs, bias, hidden, q_ref, res_ref, sem = rest[BLOCKS:]
    q_in = pltpu.make_async_copy(q_hbm, q_ref, sem.at[0])
    res_in = pltpu.make_async_copy(res_hbm, res_ref, sem.at[1])
    q_in.start()
    res_in.start()
    x, zh, c = where_ref[0], where_ref[1], where_ref[2]
    index = 0
    for back in (2, 1, 0):
        for other_zh in (0, 1):
            for other_c in (0, 1):
                zh_at = zh if other_zh == 0 else 1 - zh
                c_at = c if other_c == 0 else 1 - c
                slot = (2 - back) * 4 + zh_at * 2 + c_at
                kv[pl.ds(pl.multiple_of(slot * TOK, TOK), TOK), :] = blocks[index][:TOK, :]
                row = blocks[index][TOK:, :TOK].astype(F32)
                segs[pl.ds(slot, 1), :] = row[:1, :]
                index += 1
    first = zh * 2 + c
    own = x * 4 + first
    mine = seg_ref[...]
    t = lax.broadcasted_iota(jnp.int32, (TOK, TOK), 0)
    s = lax.broadcasted_iota(jnp.int32, (TOK, TOK), 1)
    for i in range(WINDOW):
        number = own - (WINDOW - 1) + i
        same = segs[pl.ds(first + i, 1), :] == mine
        allowed = same & (number >= 0)
        if i == WINDOW - 1:
            allowed = allowed & (s <= t)
        bias[:, i * TOK : (i + 1) * TOK] = jnp.where(allowed, 0.0, -1e30)
    start = pl.multiple_of(first * TOK, TOK)
    rate = HD ** (-0.5) * 1.4426950408889634
    q_in.wait()
    res_in.wait()
    for g in range(KVH):
        key = kv[pl.ds(start, WINDOW * TOK), g * HD : (g + 1) * HD]
        value = kv[pl.ds(start, WINDOW * TOK), (KVH + g) * HD : (KVH + g + 1) * HD]
        for j in range(GROUPS):
            columns = slice((g * GROUPS + j) * HD, (g * GROUPS + j + 1) * HD)
            score = lax.dot_general(q_ref[:, columns], key, NT, preferred_element_type=F32)
            score = score + bias[...]
            peak = jnp.max(score, axis=-1, keepdims=True)
            weight = jnp.exp2((score - peak) * rate)
            total = jnp.sum(weight, axis=-1, keepdims=True)
            mixed = jnp.dot(weight.astype(BF16), value, preferred_element_type=F32)
            hidden[:, columns] = res_ref[:, columns].astype(F32) + mixed / total
    full = hidden[...]
    hidden_ref[...] = full
    mean = jnp.mean(full * full, axis=-1, keepdims=True)
    normed = (full * lax.rsqrt(mean + 1e-6) * gain_ref[...].astype(F32)).astype(BF16)
    for n in range(0, D, 512):
        out_ref[:, n : n + 512] = jnp.dot(
            send_ref[...], normed[:, n : n + 512], preferred_element_type=F32
        ).astype(BF16)


def attention(where, q, seg, res, gain, send, blocks):
    whole = pl.BlockSpec(memory_space=pltpu.VMEM)
    hbm = pl.BlockSpec(memory_space=pl.ANY)
    return pl.pallas_call(
        attention_kernel,
        in_specs=[pl.BlockSpec(memory_space=pltpu.SMEM), hbm, whole, hbm] + [whole] * (2 + BLOCKS),
        out_specs=(whole, whole),
        out_shape=(
            jax.ShapeDtypeStruct((TOK, D), F32),
            jax.ShapeDtypeStruct((SLOTS, D), BF16),
        ),
        scratch_shapes=[
            pltpu.VMEM((BLOCKS * TOK, 2 * KVH * HD), BF16),
            pltpu.VMEM((16, TOK), F32),
            pltpu.VMEM((TOK, WINDOW * TOK), F32),
            pltpu.VMEM((TOK, D), F32),
            pltpu.VMEM((TOK, D), BF16),
            pltpu.VMEM((TOK, D), BF16),
            pltpu.SemaphoreType.DMA((2,)),
        ],
        compiler_params=params(48),
        cost_estimate=pl.CostEstimate(
            flops=1_900_000_000, bytes_accessed=9_000_000, transcendentals=2_400_000
        ),
        name="attend",
    )(where, q, seg, res, gain, send, *blocks)


def slice_place(expert, x, zh, c):
    return (expert + 8 * zh + (x - 4 if c == 0 else 3 - x)) % 16


STEP = 576


def expert_kernel(where_ref, x_hbm, w_hbm, out_hbm, x_ref, w_ref, out_ref, sem_x, sem_w, sem_out):
    x = where_ref[0]
    chunks = range(0, SLOTS, STEP)

    def rows_in(i):
        at = pl.ds(i * STEP, STEP)
        return pltpu.make_async_copy(x_hbm.at[at], x_ref.at[at], sem_x.at[i])

    def rows_out(i):
        at = pl.ds(i * STEP, STEP)
        return pltpu.make_async_copy(out_ref.at[at], out_hbm.at[at], sem_out.at[i])

    def weight_slice(which, k):
        place = slice_place(2 * x + which, k // 4, (k // 2) % 2, k % 2)
        at = pl.ds(pl.multiple_of((which * 16 + place) * TOK, TOK), TOK)
        return pltpu.make_async_copy(
            w_hbm.at[at], w_ref.at[which, pl.ds(k * TOK, TOK)], sem_w.at[which, k]
        )

    rows_in(0).start()
    for which in (0, 1):
        for k in range(16):
            weight_slice(which, k).start()
        if which == 0:
            for i in range(1, len(chunks)):
                rows_in(i).start()

    def run(rows, which):
        gate_up = jnp.dot(rows, w_ref[which, :, : 2 * FF], preferred_element_type=F32)
        gate, up = gate_up[:, :FF], gate_up[:, FF:]
        inner = (gate * jax.nn.sigmoid(gate) * up).astype(BF16)
        return lax.dot_general(
            inner, w_ref[which, :, 2 * FF :], NT, preferred_element_type=F32
        ).astype(BF16)

    line = lax.broadcasted_iota(jnp.int32, (16, 1), 0)
    for which in (0, 1):
        for k in range(16):
            weight_slice(which, k).wait()
        for i, chunk in enumerate(chunks):
            starts = range(chunk, chunk + STEP, 144)
            if which == 0:
                rows_in(i).wait()
                rows = [x_ref[a + b : a + b + 48, :] for a in starts for b in (0, 96)]
                y = run(jnp.concatenate(rows, axis=0), 0)
                for n, a in enumerate(starts):
                    out_ref[a : a + 48, :] = y[n * 96 : n * 96 + 48]
                    out_ref[a + 96 : a + 144, :] = y[n * 96 + 48 : n * 96 + 96]
            else:
                y = run(jnp.concatenate([x_ref[a + 32 : a + 112, :] for a in starts], axis=0), 1)
                for n, a in enumerate(starts):
                    p = y[n * 80 : n * 80 + 80]
                    head, tail = out_ref[a + 32 : a + 48, :], out_ref[a + 96 : a + 112, :]
                    out_ref[a + 32 : a + 48, :] = jnp.where(line < 4, head, p[:16])
                    out_ref[a + 48 : a + 96, :] = p[16:64]
                    out_ref[a + 96 : a + 112, :] = jnp.where(line < 12, p[64:], tail)
                rows_out(i).start()
    for i in range(len(chunks)):
        rows_out(i).wait()


def experts(where, x, both):
    hbm = pl.BlockSpec(memory_space=pl.ANY)
    return pl.pallas_call(
        expert_kernel,
        in_specs=[pl.BlockSpec(memory_space=pltpu.SMEM), hbm, hbm],
        out_specs=hbm,
        out_shape=jax.ShapeDtypeStruct((SLOTS, D), BF16),
        scratch_shapes=[
            pltpu.VMEM((SLOTS, D), BF16),
            pltpu.VMEM((2, D, 3 * FF), BF16),
            pltpu.VMEM((SLOTS, D), BF16),
            pltpu.SemaphoreType.DMA((SLOTS // STEP,)),
            pltpu.SemaphoreType.DMA((2, 16)),
            pltpu.SemaphoreType.DMA((SLOTS // STEP,)),
        ],
        compiler_params=params(56),
        cost_estimate=pl.CostEstimate(
            flops=6_600_000_000, bytes_accessed=19_000_000, transcendentals=540_000
        ),
        name="expert_mlp",
    )(where, x, both)


def combine_kernel(hidden_ref, high_ref, low_ref, back_ref, out_ref):
    back = back_ref[...]
    routed = jnp.dot(high_ref[...], back, preferred_element_type=F32)
    routed = routed + jnp.dot(low_ref[...], back, preferred_element_type=F32)
    out_ref[...] = (hidden_ref[...] + routed).astype(BF16)


def combine(hidden, high, low, back):
    wide = 512
    return pl.pallas_call(
        combine_kernel,
        grid=(D // wide,),
        in_specs=[
            pl.BlockSpec((TOK, wide), lambda i: (0, i)),
            pl.BlockSpec((TOK, SLOTS), lambda i: (0, 0)),
            pl.BlockSpec((TOK, SLOTS), lambda i: (0, 0)),
            pl.BlockSpec((SLOTS, wide), lambda i: (0, i)),
        ],
        out_specs=pl.BlockSpec((TOK, wide), lambda i: (0, i)),
        out_shape=jax.ShapeDtypeStruct((TOK, D), BF16),
        compiler_params=params(32),
        cost_estimate=pl.CostEstimate(
            flops=1_200_000_000, bytes_accessed=7_000_000, transcendentals=0
        ),
        name="combine",
    )(hidden, high, low, back)


def shifted(steps, swap):
    return [
        (x * 2 + c, (x + steps) * 2 + (c ^ swap)) for x in range(4) for c in range(2) if x + steps < 4
    ]


def to_expert_column():
    pairs = []
    for k in range(16):
        for zl in range(8):
            place = slice_place(zl, k // 4, (k // 2) % 2, k % 2)
            target = ((zl // 2 * 2 + place // 8) * 2 + zl % 2) * 8 + place % 8
            pairs.append((k * 8 + zl, target))
    return pairs


def body(q, k, v, seg, res, gain, ids, gates, w_gate, w_up, w_down):
    x, zh, c, y = (lax.axis_index(a) for a in ("x", "zh", "c", "y"))
    swap = [(0, 1), (1, 0)]

    seg_rows = jnp.pad(seg.astype(BF16), ((0, PACK - TOK - 1), (0, 2 * KVH * HD - TOK)))
    packet = jnp.concatenate([jnp.concatenate([k[0], v[0]], axis=1), seg_rows], axis=0)
    def spread(source):
        found = [[source, lax.ppermute(source, "c", swap)]]
        for back in (1, 2):
            found.append([lax.ppermute(source, ("x", "c"), shifted(back, o)) for o in (0, 1)])
        return found

    packet_zh = lax.ppermute(packet, "zh", swap)
    near = spread(packet)
    packed = jnp.concatenate([w_gate[0], w_up[0], w_down[0].T], axis=1)
    packed = lax.ppermute(packed, ("x", "zh", "c", "zl"), to_expert_column())
    packed, packet_zh, near = lax.optimization_barrier((packed, packet_zh, near))
    both = lax.all_gather(packed, ("c", "zh", "zl"), axis=0, tiled=True)
    far = spread(packet_zh)
    blocks = [side[b][o] for b in (2, 1, 0) for side in (near, far) for o in (0, 1)]

    e = ids[0]
    half = (e & 1) ^ (y & 1)
    order = ((e >> 1) & 3) * 8 + (e >> 3) * 2 + half
    send, high, low = slot_matrices(order, gates[0])

    where = jnp.stack([x, zh, c]).astype(jnp.int32)
    hidden, outgoing = attention(
        where, q[0], seg[0].astype(F32)[:, None], res[0], gain[None], send, blocks
    )
    arrived = lax.all_to_all(outgoing, ("x", "y"), 0, 0, tiled=True)
    done = experts(where, arrived, both)
    back = lax.all_to_all(done, ("x", "y"), 0, 0, tiled=True)
    return combine(hidden, high, low, back)[None]


def solution(mesh):
    fine = Mesh(mesh.devices.reshape(4, 2, 2, 4, 8), AXES)
    exp, ctx = ("y", "zl"), ("x", "zh", "c")
    rows = P(exp, ctx, None)
    return jax.shard_map(
        body,
        mesh=fine,
        in_specs=(rows, rows, rows, P(exp, ctx), rows, P(), rows, rows, rows, rows, P(exp, None, ctx)),
        out_specs=rows,
        check_vma=False,
    )
```

```python
import functools

import jax
import jax.numpy as jnp
from jax import lax
from jax.experimental import pallas as pl
from jax.experimental.pallas import tpu as pltpu
from jax.sharding import Mesh, PartitionSpec as P

D = 2048
HEADS = 16
KVH = 2
GROUPS = HEADS // KVH
HD = 128
FF = 384
EXPERTS = 32
TOPK = 8
TOK = 128
CAP = 36
SLOTS = EXPERTS * CAP
PACK = 144
WINDOW = 9
BLOCKS = 12
AXES = ("x", "zh", "c", "y", "zl")
F32 = jnp.float32
BF16 = jnp.bfloat16
NT = (((1,), (1,)), ((), ()))


def params(mib):
    return pltpu.CompilerParams(vmem_limit_bytes=mib * 1024 * 1024)


def slot_kernel(where_ref, ids_ref, gates_ref, send_ref, high_ref, low_ref):
    e = ids_ref[...]
    half = (e & 1) ^ (where_ref[3] & 1)
    ids = ((e >> 1) & 3) * 8 + (e >> 3) * 2 + half
    gates = gates_ref[...]
    line = lax.broadcasted_iota(jnp.int32, (EXPERTS, TOK), 0)
    named = jnp.zeros((EXPERTS, TOK), F32)
    gate = jnp.zeros((EXPERTS, TOK), F32)
    for k in range(TOPK):
        hit = ids[k : k + 1, :] == line
        named = named + jnp.where(hit, 1.0, 0.0)
        gate = gate + jnp.where(hit, gates[k : k + 1, :], 0.0)
    row = lax.broadcasted_iota(jnp.int32, (TOK, TOK), 0)
    earlier = (row < lax.broadcasted_iota(jnp.int32, (TOK, TOK), 1)).astype(F32).astype(BF16)
    rank = jnp.dot(named.astype(BF16), earlier, preferred_element_type=F32)
    rank = jnp.where(named > 0.0, rank, -1.0)
    slot = lax.broadcasted_iota(jnp.int32, (SLOTS, EXPERTS), 0).astype(F32)
    owner = jnp.floor((slot + 0.5) * (1.0 / CAP))
    place = slot - CAP * owner
    expert = lax.broadcasted_iota(jnp.int32, (SLOTS, EXPERTS), 1).astype(F32)
    spread = jnp.where(owner == expert, 1.0, 0.0).astype(BF16)
    rank_rows = jnp.dot(spread, rank.astype(BF16), preferred_element_type=F32)
    send_ref[...] = jnp.where(rank_rows == place[:, :1], 1.0, 0.0).astype(BF16)
    slot_t = lax.broadcasted_iota(jnp.int32, (1, SLOTS), 1).astype(F32)
    place_t = slot_t - CAP * jnp.floor((slot_t + 0.5) * (1.0 / CAP))
    rank_t = jnp.transpose(rank).astype(BF16)
    taken = lax.dot_general(rank_t, spread, NT, preferred_element_type=F32) == place_t
    gate = jnp.transpose(gate)
    high = gate.astype(BF16)
    low = (gate - high.astype(F32)).astype(BF16)
    for part, ref in ((high, high_ref), (low, low_ref)):
        wide = lax.dot_general(part, spread, NT, preferred_element_type=F32)
        ref[...] = jnp.where(taken, wide, 0.0).astype(BF16)


def slot_matrices(where, ids, gates):
    whole = pl.BlockSpec(memory_space=pltpu.VMEM)
    return pl.pallas_call(
        slot_kernel,
        in_specs=[pl.BlockSpec(memory_space=pltpu.SMEM)] + [whole] * 2,
        out_specs=(whole,) * 3,
        out_shape=(
            jax.ShapeDtypeStruct((SLOTS, TOK), BF16),
            jax.ShapeDtypeStruct((TOK, SLOTS), BF16),
            jax.ShapeDtypeStruct((TOK, SLOTS), BF16),
        ),
        compiler_params=params(16),
        cost_estimate=pl.CostEstimate(flops=40_000_000, bytes_accessed=1_000_000, transcendentals=0),
        name="slots",
    )(where, ids, gates)


def attention_kernel(where_ref, q_ref, seg_ref, res_ref, gain_ref, send_ref, *rest):
    blocks = rest[:BLOCKS]
    hidden_ref, out_ref, kv, segs, bias, hidden = rest[BLOCKS:]
    x, zh, c = where_ref[0], where_ref[1], where_ref[2]
    index = 0
    for back in (2, 1, 0):
        for other_zh in (0, 1):
            for other_c in (0, 1):
                zh_at = zh if other_zh == 0 else 1 - zh
                c_at = c if other_c == 0 else 1 - c
                slot = (2 - back) * 4 + zh_at * 2 + c_at
                kv[pl.ds(pl.multiple_of(slot * TOK, TOK), TOK), :] = blocks[index][:TOK, :]
                row = blocks[index][TOK:, :TOK].astype(F32)
                segs[pl.ds(slot, 1), :] = row[:1, :]
                index += 1
    first = zh * 2 + c
    own = x * 4 + first
    t = lax.broadcasted_iota(jnp.int32, (TOK, TOK), 0)
    s = lax.broadcasted_iota(jnp.int32, (TOK, TOK), 1)
    mine = jnp.sum(jnp.where(s == t, seg_ref[...].astype(F32), 0.0), axis=1, keepdims=True)
    for i in range(WINDOW):
        number = own - (WINDOW - 1) + i
        same = segs[pl.ds(first + i, 1), :] == mine
        allowed = same & (number >= 0)
        if i == WINDOW - 1:
            allowed = allowed & (s <= t)
        bias[:, i * TOK : (i + 1) * TOK] = jnp.where(allowed, 0.0, -1e30)
    start = pl.multiple_of(first * TOK, TOK)
    rate = HD ** (-0.5) * 1.4426950408889634
    for g in range(KVH):
        key = kv[pl.ds(start, WINDOW * TOK), g * HD : (g + 1) * HD]
        value = kv[pl.ds(start, WINDOW * TOK), (KVH + g) * HD : (KVH + g + 1) * HD]
        for j in range(GROUPS):
            columns = slice((g * GROUPS + j) * HD, (g * GROUPS + j + 1) * HD)
            score = lax.dot_general(q_ref[:, columns], key, NT, preferred_element_type=F32)
            score = score + bias[...]
            peak = jnp.max(score, axis=-1, keepdims=True)
            weight = jnp.exp2((score - peak) * rate)
            total = jnp.sum(weight, axis=-1, keepdims=True)
            mixed = jnp.dot(weight.astype(BF16), value, preferred_element_type=F32)
            hidden[:, columns] = res_ref[:, columns].astype(F32) + mixed / total
    full = hidden[...]
    hidden_ref[...] = full
    mean = jnp.mean(full * full, axis=-1, keepdims=True)
    normed = (full * lax.rsqrt(mean + 1e-6) * gain_ref[...].astype(F32)).astype(BF16)
    for n in range(0, D, 512):
        out_ref[:, n : n + 512] = jnp.dot(
            send_ref[...], normed[:, n : n + 512], preferred_element_type=F32
        ).astype(BF16)


def attention(where, q, seg, res, gain, send, blocks):
    whole = pl.BlockSpec(memory_space=pltpu.VMEM)
    return pl.pallas_call(
        attention_kernel,
        in_specs=[pl.BlockSpec(memory_space=pltpu.SMEM)] + [whole] * (5 + BLOCKS),
        out_specs=(whole, whole),
        out_shape=(
            jax.ShapeDtypeStruct((TOK, D), F32),
            jax.ShapeDtypeStruct((SLOTS, D), BF16),
        ),
        scratch_shapes=[
            pltpu.VMEM((BLOCKS * TOK, 2 * KVH * HD), BF16),
            pltpu.VMEM((16, TOK), F32),
            pltpu.VMEM((TOK, WINDOW * TOK), F32),
            pltpu.VMEM((TOK, D), F32),
        ],
        compiler_params=params(20),
        cost_estimate=pl.CostEstimate(
            flops=1_900_000_000, bytes_accessed=9_000_000, transcendentals=2_400_000
        ),
        name="attend",
    )(where, q, seg, res, gain, send, *blocks)


def slice_place(expert, x, zh, c):
    return (expert + 8 * zh + (x - 4 if c == 0 else 3 - x)) % 16


STEP = 576


def expert_kernel(where_ref, x_ref, w_hbm, out_ref, w_ref, down_ref, sem_w):
    x = where_ref[0]
    chunks = range(0, SLOTS, STEP)

    def source(which, k):
        place = slice_place(2 * x + which, k // 4, (k // 2) % 2, k % 2)
        return pl.ds(pl.multiple_of((which * 16 + place) * TOK, TOK), TOK)

    def weight_slice(which, k):
        return pltpu.make_async_copy(
            w_hbm.at[source(which, k)], w_ref.at[which, pl.ds(k * TOK, TOK)], sem_w.at[which, k]
        )

    def start(which, half):
        for k in range(half * 8, half * 8 + 8):
            weight_slice(which, k).start()

    def wait(which, half):
        for k in range(half * 8, half * 8 + 8):
            weight_slice(which, k).wait()

    start(0, 0)
    start(0, 1)

    def run(which, spans, first):
        def rows(columns):
            return jnp.concatenate([x_ref[a:b, columns] for a, b in spans], axis=0)

        gate_up = None
        if first:
            for half in (0, 1):
                wait(which, half)
                if which == 0:
                    start(1, half)
                for j in range(0, FF, TOK):
                    for k in range(half * 8, half * 8 + 8):
                        down_ref[which, j : j + TOK, k * TOK : (k + 1) * TOK] = w_ref[
                            which, k * TOK : (k + 1) * TOK, 2 * FF + j : 2 * FF + j + TOK
                        ]
                if which == 0:
                    part = slice(half * 1024, half * 1024 + 1024)
                    term = jnp.dot(
                        rows(part), w_ref[which, part, : 2 * FF], preferred_element_type=F32
                    )
                    gate_up = term if gate_up is None else gate_up + term
        if gate_up is None:
            gate_up = jnp.dot(
                rows(slice(0, D)), w_ref[which, :, : 2 * FF], preferred_element_type=F32
            )
        gate, up = gate_up[:, :FF], gate_up[:, FF:]
        near = 0.5 * gate
        inner = ((near + near * jnp.tanh(near)) * up).astype(BF16)
        return jnp.dot(inner, down_ref[which], preferred_element_type=F32).astype(BF16)

    line = lax.broadcasted_iota(jnp.int32, (16, 1), 0)
    for which in (0, 1):
        for i, chunk in enumerate(chunks):
            starts = range(chunk, chunk + STEP, 144)
            if which == 0:
                y = run(0, [(a + b, a + b + 48) for a in starts for b in (0, 96)], i == 0)
                for n, a in enumerate(starts):
                    out_ref[a : a + 48, :] = y[n * 96 : n * 96 + 48]
                    out_ref[a + 96 : a + 144, :] = y[n * 96 + 48 : n * 96 + 96]
            else:
                y = run(1, [(a + 32, a + 112) for a in starts], i == 0)
                for n, a in enumerate(starts):
                    p = y[n * 80 : n * 80 + 80]
                    head, tail = out_ref[a + 32 : a + 48, :], out_ref[a + 96 : a + 112, :]
                    out_ref[a + 32 : a + 48, :] = jnp.where(line < 4, head, p[:16])
                    out_ref[a + 48 : a + 96, :] = p[16:64]
                    out_ref[a + 96 : a + 112, :] = jnp.where(line < 12, p[64:], tail)


def experts(where, x, both):
    hbm = pl.BlockSpec(memory_space=pltpu.HBM)
    whole = pl.BlockSpec(memory_space=pltpu.VMEM)
    return pl.pallas_call(
        expert_kernel,
        in_specs=[pl.BlockSpec(memory_space=pltpu.SMEM), whole, hbm],
        out_specs=whole,
        out_shape=jax.ShapeDtypeStruct((SLOTS, D), BF16),
        scratch_shapes=[
            pltpu.VMEM((2, D, 3 * FF), BF16),
            pltpu.VMEM((2, FF, D), BF16),
            pltpu.SemaphoreType.DMA((2, 16)),
        ],
        compiler_params=params(44),
        cost_estimate=pl.CostEstimate(
            flops=6_600_000_000, bytes_accessed=19_000_000, transcendentals=540_000
        ),
        name="expert_mlp",
    )(where, x, both)


def combine_kernel(hidden_ref, high_ref, low_ref, back_ref, out_ref):
    back = back_ref[...]
    routed = jnp.dot(high_ref[...], back, preferred_element_type=F32)
    routed = routed + jnp.dot(low_ref[...], back, preferred_element_type=F32)
    out_ref[...] = (hidden_ref[...] + routed).astype(BF16)


def combine(hidden, high, low, back):
    wide = 512
    return pl.pallas_call(
        combine_kernel,
        grid=(D // wide,),
        in_specs=[
            pl.BlockSpec((TOK, wide), lambda i: (0, i)),
            pl.BlockSpec((TOK, SLOTS), lambda i: (0, 0)),
            pl.BlockSpec((TOK, SLOTS), lambda i: (0, 0)),
            pl.BlockSpec((SLOTS, wide), lambda i: (0, i)),
        ],
        out_specs=pl.BlockSpec((TOK, wide), lambda i: (0, i)),
        out_shape=jax.ShapeDtypeStruct((TOK, D), BF16),
        compiler_params=params(16),
        cost_estimate=pl.CostEstimate(
            flops=1_200_000_000, bytes_accessed=7_000_000, transcendentals=0
        ),
        name="combine",
    )(hidden, high, low, back)


def shifted(steps, swap):
    return [
        (x * 2 + c, (x + steps) * 2 + (c ^ swap)) for x in range(4) for c in range(2) if x + steps < 4
    ]


def to_expert_column():
    pairs = []
    for k in range(16):
        for zl in range(8):
            place = slice_place(zl, k // 4, (k // 2) % 2, k % 2)
            target = ((zl // 2 * 2 + place // 8) * 2 + zl % 2) * 8 + place % 8
            pairs.append((k * 8 + zl, target))
    return pairs


def body(q, k, v, seg, res, gain, ids, gates, w_gate, w_up, w_down):
    x, zh, c, y = (lax.axis_index(a) for a in ("x", "zh", "c", "y"))
    swap = [(0, 1), (1, 0)]

    seg_rows = jnp.pad(seg.astype(BF16), ((0, PACK - TOK - 1), (0, 2 * KVH * HD - TOK)))
    packet = jnp.concatenate([jnp.concatenate([k[0], v[0]], axis=1), seg_rows], axis=0)

    def spread(source):
        found = [[source, lax.ppermute(source, "c", swap)]]
        for back in (1, 2):
            found.append([lax.ppermute(source, ("x", "c"), shifted(back, o)) for o in (0, 1)])
        return found

    packet_zh = lax.ppermute(packet, "zh", swap)
    near = spread(packet)
    down = [w_down[0, j : j + TOK] for j in range(0, FF, TOK)]
    packed = jnp.concatenate([w_gate[0], w_up[0], *down], axis=1)
    packed, packet_zh, near = lax.optimization_barrier((packed, packet_zh, near))
    far = spread(packet_zh)
    packed = lax.ppermute(packed, ("x", "zh", "c", "zl"), to_expert_column())
    where = jnp.stack([x, zh, c, y]).astype(jnp.int32)
    ready = (*slot_matrices(where, ids[0].T, gates[0].T), gain[None], seg)
    packed, far, ready = lax.optimization_barrier((packed, far, ready))
    both = lax.all_gather(packed, ("c", "zh", "zl"), axis=0, tiled=True)
    blocks = [side[b][o] for b in (2, 1, 0) for side in (near, far) for o in (0, 1)]

    send, high, low, gain_row, seg_row = ready
    hidden, outgoing = attention(where, q[0], seg_row, res[0], gain_row, send, blocks)
    arrived = lax.all_to_all(outgoing, ("x", "y"), 0, 0, tiled=True)
    done = experts(where, arrived, both)
    back = lax.all_to_all(done, ("x", "y"), 0, 0, tiled=True)
    return combine(hidden, high, low, back)[None]


def solution(mesh):
    fine = Mesh(mesh.devices.reshape(4, 2, 2, 4, 8), AXES)
    exp, ctx = ("y", "zl"), ("x", "zh", "c")
    rows = P(exp, ctx, None)
    return jax.shard_map(
        body,
        mesh=fine,
        in_specs=(rows, rows, rows, P(exp, ctx), rows, P(), rows, rows, rows, rows, P(exp, None, ctx)),
        out_specs=rows,
        check_vma=False,
    )
```

```python
import functools

import jax
import jax.numpy as jnp
from jax import lax
from jax.experimental import pallas as pl
from jax.experimental.pallas import tpu as pltpu
from jax.sharding import Mesh, PartitionSpec as P

D = 2048
HEADS = 16
KVH = 2
GROUPS = HEADS // KVH
HD = 128
FF = 384
EXPERTS = 32
TOPK = 8
TOK = 128
CAP = 36
SLOTS = EXPERTS * CAP
PACK = 144
WINDOW = 9
BLOCKS = 12
AXES = ("x", "zh", "c", "y", "zl")
F32 = jnp.float32
BF16 = jnp.bfloat16
NT = (((1,), (1,)), ((), ()))


def params(mib):
    return pltpu.CompilerParams(vmem_limit_bytes=mib * 1024 * 1024)


def pack_kernel(k_in, v_in, gate_in, up_in, down_in, seg_ref, packet_ref, packed_ref, sem):
    pieces = [
        (gate_in, packed_ref.at[:, pl.ds(0, FF)]),
        (up_in, packed_ref.at[:, pl.ds(FF, FF)]),
        (k_in, packet_ref.at[pl.ds(0, TOK), pl.ds(0, KVH * HD)]),
        (v_in, packet_ref.at[pl.ds(0, TOK), pl.ds(KVH * HD, KVH * HD)]),
    ]
    for j in range(0, FF, TOK):
        pieces.append((down_in.at[pl.ds(j, TOK)], packed_ref.at[:, pl.ds(2 * FF + j, TOK)]))
    copies = [pltpu.make_async_copy(a, b, sem.at[n]) for n, (a, b) in enumerate(pieces)]
    for copy in copies:
        copy.start()
    line = lax.broadcasted_iota(jnp.int32, (PACK - TOK, TOK), 0)
    row = jnp.where(line == 0, seg_ref[...].astype(F32), 0.0)
    packet_ref[TOK:, :TOK] = row.astype(BF16)
    packet_ref[TOK:, TOK:] = jnp.zeros((PACK - TOK, 2 * KVH * HD - TOK), BF16)
    for copy in copies:
        copy.wait()


def pack(k, v, w_gate, w_up, w_down, seg):
    whole = pl.BlockSpec(memory_space=pltpu.VMEM)
    return pl.pallas_call(
        pack_kernel,
        in_specs=[pl.BlockSpec(memory_space=pl.ANY)] * 5 + [whole],
        out_specs=(whole, whole),
        out_shape=(
            jax.ShapeDtypeStruct((PACK, 2 * KVH * HD), BF16),
            jax.ShapeDtypeStruct((TOK, 3 * FF), BF16),
        ),
        scratch_shapes=[pltpu.SemaphoreType.DMA((4 + FF // TOK,))],
        compiler_params=params(56),
        cost_estimate=pl.CostEstimate(flops=0, bytes_accessed=1_000_000, transcendentals=0),
        name="pack",
    )(k, v, w_gate, w_up, w_down, seg)


def slot_kernel(where_ref, ids_ref, gates_ref, send_ref, high_ref, low_ref):
    e = ids_ref[...]
    half = (e & 1) ^ (where_ref[3] & 1)
    ids = ((e >> 1) & 3) * 8 + (e >> 3) * 2 + half
    gates = gates_ref[...]
    line = lax.broadcasted_iota(jnp.int32, (EXPERTS, TOK), 0)
    named = jnp.zeros((EXPERTS, TOK), F32)
    gate = jnp.zeros((EXPERTS, TOK), F32)
    for k in range(TOPK):
        hit = ids[k : k + 1, :] == line
        named = named + jnp.where(hit, 1.0, 0.0)
        gate = gate + jnp.where(hit, gates[k : k + 1, :], 0.0)
    row = lax.broadcasted_iota(jnp.int32, (TOK, TOK), 0)
    earlier = (row < lax.broadcasted_iota(jnp.int32, (TOK, TOK), 1)).astype(F32).astype(BF16)
    rank = jnp.dot(named.astype(BF16), earlier, preferred_element_type=F32)
    rank = jnp.where(named > 0.0, rank, -1.0)
    slot = lax.broadcasted_iota(jnp.int32, (SLOTS, EXPERTS), 0).astype(F32)
    owner = jnp.floor((slot + 0.5) * (1.0 / CAP))
    place = slot - CAP * owner
    expert = lax.broadcasted_iota(jnp.int32, (SLOTS, EXPERTS), 1).astype(F32)
    spread = jnp.where(owner == expert, 1.0, 0.0).astype(BF16)
    rank_rows = jnp.dot(spread, rank.astype(BF16), preferred_element_type=F32)
    send_ref[...] = jnp.where(rank_rows == place[:, :1], 1.0, 0.0).astype(BF16)
    slot_t = lax.broadcasted_iota(jnp.int32, (1, SLOTS), 1).astype(F32)
    place_t = slot_t - CAP * jnp.floor((slot_t + 0.5) * (1.0 / CAP))
    rank_t = jnp.transpose(rank).astype(BF16)
    taken = lax.dot_general(rank_t, spread, NT, preferred_element_type=F32) == place_t
    gate = jnp.transpose(gate)
    high = gate.astype(BF16)
    low = (gate - high.astype(F32)).astype(BF16)
    for part, ref in ((high, high_ref), (low, low_ref)):
        wide = lax.dot_general(part, spread, NT, preferred_element_type=F32)
        ref[...] = jnp.where(taken, wide, 0.0).astype(BF16)


def slot_matrices(where, ids, gates):
    whole = pl.BlockSpec(memory_space=pltpu.VMEM)
    return pl.pallas_call(
        slot_kernel,
        in_specs=[pl.BlockSpec(memory_space=pltpu.SMEM)] + [whole] * 2,
        out_specs=(whole,) * 3,
        out_shape=(
            jax.ShapeDtypeStruct((SLOTS, TOK), BF16),
            jax.ShapeDtypeStruct((TOK, SLOTS), BF16),
            jax.ShapeDtypeStruct((TOK, SLOTS), BF16),
        ),
        compiler_params=params(16),
        cost_estimate=pl.CostEstimate(flops=40_000_000, bytes_accessed=1_000_000, transcendentals=0),
        name="slots",
    )(where, ids, gates)


def attention_kernel(where_ref, q_ref, seg_ref, res_ref, gain_ref, send_ref, *rest):
    blocks = rest[:BLOCKS]
    hidden_ref, out_ref, kv, segs, bias, hidden = rest[BLOCKS:]
    x, zh, c = where_ref[0], where_ref[1], where_ref[2]
    index = 0
    for back in (2, 1, 0):
        for other_zh in (0, 1):
            for other_c in (0, 1):
                zh_at = zh if other_zh == 0 else 1 - zh
                c_at = c if other_c == 0 else 1 - c
                slot = (2 - back) * 4 + zh_at * 2 + c_at
                kv[pl.ds(pl.multiple_of(slot * TOK, TOK), TOK), :] = blocks[index][:TOK, :]
                row = blocks[index][TOK:, :TOK].astype(F32)
                segs[pl.ds(slot, 1), :] = row[:1, :]
                index += 1
    first = zh * 2 + c
    own = x * 4 + first
    t = lax.broadcasted_iota(jnp.int32, (TOK, TOK), 0)
    s = lax.broadcasted_iota(jnp.int32, (TOK, TOK), 1)
    mine = jnp.sum(jnp.where(s == t, seg_ref[...].astype(F32), 0.0), axis=1, keepdims=True)
    for i in range(WINDOW):
        number = own - (WINDOW - 1) + i
        same = segs[pl.ds(first + i, 1), :] == mine
        allowed = same & (number >= 0)
        if i == WINDOW - 1:
            allowed = allowed & (s <= t)
        bias[:, i * TOK : (i + 1) * TOK] = jnp.where(allowed, 0.0, -1e30)
    start = pl.multiple_of(first * TOK, TOK)
    rate = HD ** (-0.5) * 1.4426950408889634
    for g in range(KVH):
        key = kv[pl.ds(start, WINDOW * TOK), g * HD : (g + 1) * HD]
        value = kv[pl.ds(start, WINDOW * TOK), (KVH + g) * HD : (KVH + g + 1) * HD]
        for j in range(GROUPS):
            columns = slice((g * GROUPS + j) * HD, (g * GROUPS + j + 1) * HD)
            score = lax.dot_general(q_ref[:, columns], key, NT, preferred_element_type=F32)
            score = score + bias[...]
            peak = jnp.max(score, axis=-1, keepdims=True)
            weight = jnp.exp2((score - peak) * rate)
            total = jnp.sum(weight, axis=-1, keepdims=True)
            mixed = jnp.dot(weight.astype(BF16), value, preferred_element_type=F32)
            hidden[:, columns] = res_ref[:, columns].astype(F32) + mixed / total
    full = hidden[...]
    hidden_ref[...] = full
    mean = jnp.mean(full * full, axis=-1, keepdims=True)
    normed = (full * lax.rsqrt(mean + 1e-6) * gain_ref[...].astype(F32)).astype(BF16)
    for n in range(0, D, 512):
        out_ref[:, n : n + 512] = jnp.dot(
            send_ref[...], normed[:, n : n + 512], preferred_element_type=F32
        ).astype(BF16)


def attention(where, q, seg, res, gain, send, blocks):
    whole = pl.BlockSpec(memory_space=pltpu.VMEM)
    return pl.pallas_call(
        attention_kernel,
        in_specs=[pl.BlockSpec(memory_space=pltpu.SMEM)] + [whole] * (5 + BLOCKS),
        out_specs=(whole, whole),
        out_shape=(
            jax.ShapeDtypeStruct((TOK, D), F32),
            jax.ShapeDtypeStruct((SLOTS, D), BF16),
        ),
        scratch_shapes=[
            pltpu.VMEM((BLOCKS * TOK, 2 * KVH * HD), BF16),
            pltpu.VMEM((16, TOK), F32),
            pltpu.VMEM((TOK, WINDOW * TOK), F32),
            pltpu.VMEM((TOK, D), F32),
        ],
        compiler_params=params(20),
        cost_estimate=pl.CostEstimate(
            flops=1_900_000_000, bytes_accessed=9_000_000, transcendentals=2_400_000
        ),
        name="attend",
    )(where, q, seg, res, gain, send, *blocks)


def slice_place(expert, x, zh, c):
    return (expert + 8 * zh + (x - 4 if c == 0 else 3 - x)) % 16


STEP = 576


def expert_kernel(where_ref, x_ref, w_hbm, out_ref, w_ref, down_ref, sem_w):
    x = where_ref[0]
    chunks = range(0, SLOTS, STEP)

    def source(which, k):
        place = slice_place(2 * x + which, k // 4, (k // 2) % 2, k % 2)
        return pl.ds(pl.multiple_of((which * 16 + place) * TOK, TOK), TOK)

    def weight_slice(which, k):
        return pltpu.make_async_copy(
            w_hbm.at[source(which, k)], w_ref.at[which, pl.ds(k * TOK, TOK)], sem_w.at[which, k]
        )

    def start(which, half):
        for k in range(half * 8, half * 8 + 8):
            weight_slice(which, k).start()

    def wait(which, half):
        for k in range(half * 8, half * 8 + 8):
            weight_slice(which, k).wait()

    start(0, 0)
    start(0, 1)

    def run(which, spans, first):
        def rows(columns):
            return jnp.concatenate([x_ref[a:b, columns] for a, b in spans], axis=0)

        gate_up = None
        if first:
            for half in (0, 1):
                wait(which, half)
                if which == 0:
                    start(1, half)
                for j in range(0, FF, TOK):
                    for k in range(half * 8, half * 8 + 8):
                        down_ref[which, j : j + TOK, k * TOK : (k + 1) * TOK] = w_ref[
                            which, k * TOK : (k + 1) * TOK, 2 * FF + j : 2 * FF + j + TOK
                        ]
                if which == 0:
                    part = slice(half * 1024, half * 1024 + 1024)
                    term = jnp.dot(
                        rows(part), w_ref[which, part, : 2 * FF], preferred_element_type=F32
                    )
                    gate_up = term if gate_up is None else gate_up + term
        if gate_up is None:
            gate_up = jnp.dot(
                rows(slice(0, D)), w_ref[which, :, : 2 * FF], preferred_element_type=F32
            )
        gate, up = gate_up[:, :FF], gate_up[:, FF:]
        near = 0.5 * gate
        inner = ((near + near * jnp.tanh(near)) * up).astype(BF16)
        return jnp.dot(inner, down_ref[which], preferred_element_type=F32).astype(BF16)

    line = lax.broadcasted_iota(jnp.int32, (16, 1), 0)
    for which in (0, 1):
        for i, chunk in enumerate(chunks):
            starts = range(chunk, chunk + STEP, 144)
            if which == 0:
                y = run(0, [(a + b, a + b + 48) for a in starts for b in (0, 96)], i == 0)
                for n, a in enumerate(starts):
                    out_ref[a : a + 48, :] = y[n * 96 : n * 96 + 48]
                    out_ref[a + 96 : a + 144, :] = y[n * 96 + 48 : n * 96 + 96]
            else:
                y = run(1, [(a + 32, a + 112) for a in starts], i == 0)
                for n, a in enumerate(starts):
                    p = y[n * 80 : n * 80 + 80]
                    head, tail = out_ref[a + 32 : a + 48, :], out_ref[a + 96 : a + 112, :]
                    out_ref[a + 32 : a + 48, :] = jnp.where(line < 4, head, p[:16])
                    out_ref[a + 48 : a + 96, :] = p[16:64]
                    out_ref[a + 96 : a + 112, :] = jnp.where(line < 12, p[64:], tail)


def experts(where, x, both):
    hbm = pl.BlockSpec(memory_space=pltpu.HBM)
    whole = pl.BlockSpec(memory_space=pltpu.VMEM)
    return pl.pallas_call(
        expert_kernel,
        in_specs=[pl.BlockSpec(memory_space=pltpu.SMEM), whole, hbm],
        out_specs=whole,
        out_shape=jax.ShapeDtypeStruct((SLOTS, D), BF16),
        scratch_shapes=[
            pltpu.VMEM((2, D, 3 * FF), BF16),
            pltpu.VMEM((2, FF, D), BF16),
            pltpu.SemaphoreType.DMA((2, 16)),
        ],
        compiler_params=params(44),
        cost_estimate=pl.CostEstimate(
            flops=6_600_000_000, bytes_accessed=19_000_000, transcendentals=540_000
        ),
        name="expert_mlp",
    )(where, x, both)


def combine_kernel(hidden_ref, high_ref, low_ref, back_ref, out_ref):
    back = back_ref[...]
    routed = jnp.dot(high_ref[...], back, preferred_element_type=F32)
    routed = routed + jnp.dot(low_ref[...], back, preferred_element_type=F32)
    out_ref[...] = (hidden_ref[...] + routed).astype(BF16)


def combine(hidden, high, low, back):
    wide = 512
    return pl.pallas_call(
        combine_kernel,
        grid=(D // wide,),
        in_specs=[
            pl.BlockSpec((TOK, wide), lambda i: (0, i)),
            pl.BlockSpec((TOK, SLOTS), lambda i: (0, 0)),
            pl.BlockSpec((TOK, SLOTS), lambda i: (0, 0)),
            pl.BlockSpec((SLOTS, wide), lambda i: (0, i)),
        ],
        out_specs=pl.BlockSpec((TOK, wide), lambda i: (0, i)),
        out_shape=jax.ShapeDtypeStruct((TOK, D), BF16),
        compiler_params=params(16),
        cost_estimate=pl.CostEstimate(
            flops=1_200_000_000, bytes_accessed=7_000_000, transcendentals=0
        ),
        name="combine",
    )(hidden, high, low, back)


def shifted(steps, swap):
    return [
        (x * 2 + c, (x + steps) * 2 + (c ^ swap)) for x in range(4) for c in range(2) if x + steps < 4
    ]


def to_expert_column():
    pairs = []
    for k in range(16):
        for zl in range(8):
            place = slice_place(zl, k // 4, (k // 2) % 2, k % 2)
            target = ((zl // 2 * 2 + place // 8) * 2 + zl % 2) * 8 + place % 8
            pairs.append((k * 8 + zl, target))
    return pairs


def body(q, k, v, seg, res, gain, ids, gates, w_gate, w_up, w_down):
    x, zh, c, y = (lax.axis_index(a) for a in ("x", "zh", "c", "y"))
    swap = [(0, 1), (1, 0)]

    packet, packed = pack(k[0], v[0], w_gate[0], w_up[0], w_down[0], seg)
    packed = lax.ppermute(packed, ("x", "zh", "c", "zl"), to_expert_column())

    def spread(source):
        found = [[source, lax.ppermute(source, "c", swap)]]
        for back in (1, 2):
            found.append([lax.ppermute(source, ("x", "c"), shifted(back, o)) for o in (0, 1)])
        return found

    packet_zh = lax.ppermute(packet, "zh", swap)
    packed, packet_near = lax.optimization_barrier((packed, packet))
    near = spread(packet_near)
    packed, packet_zh, near = lax.optimization_barrier((packed, packet_zh, near))
    both = lax.all_gather(packed, ("c", "zh", "zl"), axis=0, tiled=True)
    far = spread(packet_zh)
    where = jnp.stack([x, zh, c, y]).astype(jnp.int32)
    ready = (*slot_matrices(where, ids[0].T, gates[0].T), gain[None], seg)
    far, ready = lax.optimization_barrier((far, ready))
    blocks = [side[b][o] for b in (2, 1, 0) for side in (near, far) for o in (0, 1)]

    send, high, low, gain_row, seg_row = ready
    hidden, outgoing = attention(where, q[0], seg_row, res[0], gain_row, send, blocks)
    arrived = lax.all_to_all(outgoing, ("x", "y"), 0, 0, tiled=True)
    done = experts(where, arrived, both)
    back = lax.all_to_all(done, ("x", "y"), 0, 0, tiled=True)
    return combine(hidden, high, low, back)[None]


def solution(mesh):
    fine = Mesh(mesh.devices.reshape(4, 2, 2, 4, 8), AXES)
    exp, ctx = ("y", "zl"), ("x", "zh", "c")
    rows = P(exp, ctx, None)
    return jax.shard_map(
        body,
        mesh=fine,
        in_specs=(rows, rows, rows, P(exp, ctx), rows, P(), rows, rows, rows, rows, P(exp, None, ctx)),
        out_specs=rows,
        check_vma=False,
    )
```

```python
import functools

import jax
import jax.numpy as jnp
from jax import lax
from jax.experimental import pallas as pl
from jax.experimental.pallas import tpu as pltpu
from jax.sharding import Mesh, PartitionSpec as P

D = 2048
HEADS = 16
KVH = 2
GROUPS = HEADS // KVH
HD = 128
FF = 384
EXPERTS = 32
TOPK = 8
TOK = 128
CAP = 36
SLOTS = EXPERTS * CAP
PACK = 144
WINDOW = 9
BLOCKS = 12
AXES = ("x", "zh", "c", "y", "zl")
F32 = jnp.float32
BF16 = jnp.bfloat16
NT = (((1,), (1,)), ((), ()))


def params(mib):
    return pltpu.CompilerParams(vmem_limit_bytes=mib * 1024 * 1024)


def pack_kernel(k_in, v_in, gate_in, up_in, down_in, seg_ref, packet_ref, packed_ref, sem):
    pieces = [
        (gate_in, packed_ref.at[:, pl.ds(0, FF)]),
        (up_in, packed_ref.at[:, pl.ds(FF, FF)]),
        (k_in, packet_ref.at[pl.ds(0, TOK), pl.ds(0, KVH * HD)]),
        (v_in, packet_ref.at[pl.ds(0, TOK), pl.ds(KVH * HD, KVH * HD)]),
    ]
    for j in range(0, FF, TOK):
        pieces.append((down_in.at[pl.ds(j, TOK)], packed_ref.at[:, pl.ds(2 * FF + j, TOK)]))
    copies = [pltpu.make_async_copy(a, b, sem.at[n]) for n, (a, b) in enumerate(pieces)]
    for copy in copies:
        copy.start()
    line = lax.broadcasted_iota(jnp.int32, (PACK - TOK, TOK), 0)
    row = jnp.where(line == 0, seg_ref[...].astype(F32), 0.0)
    packet_ref[TOK:, :TOK] = row.astype(BF16)
    packet_ref[TOK:, TOK:] = jnp.zeros((PACK - TOK, 2 * KVH * HD - TOK), BF16)
    for copy in copies:
        copy.wait()


def pack(k, v, w_gate, w_up, w_down, seg):
    whole = pl.BlockSpec(memory_space=pltpu.VMEM)
    return pl.pallas_call(
        pack_kernel,
        in_specs=[pl.BlockSpec(memory_space=pl.ANY)] * 5 + [whole],
        out_specs=(whole, whole),
        out_shape=(
            jax.ShapeDtypeStruct((PACK, 2 * KVH * HD), BF16),
            jax.ShapeDtypeStruct((TOK, 3 * FF), BF16),
        ),
        scratch_shapes=[pltpu.SemaphoreType.DMA((4 + FF // TOK,))],
        compiler_params=params(56),
        cost_estimate=pl.CostEstimate(flops=0, bytes_accessed=1_000_000, transcendentals=0),
        name="pack",
    )(k, v, w_gate, w_up, w_down, seg)


def slot_kernel(where_ref, ids_ref, gates_ref, send_ref, high_ref, low_ref):
    e = ids_ref[...]
    half = (e & 1) ^ (where_ref[3] & 1)
    ids = ((e >> 1) & 3) * 8 + (e >> 3) * 2 + half
    gates = gates_ref[...]
    line = lax.broadcasted_iota(jnp.int32, (EXPERTS, TOK), 0)
    named = jnp.zeros((EXPERTS, TOK), F32)
    gate = jnp.zeros((EXPERTS, TOK), F32)
    for k in range(TOPK):
        hit = ids[k : k + 1, :] == line
        named = named + jnp.where(hit, 1.0, 0.0)
        gate = gate + jnp.where(hit, gates[k : k + 1, :], 0.0)
    row = lax.broadcasted_iota(jnp.int32, (TOK, TOK), 0)
    earlier = (row < lax.broadcasted_iota(jnp.int32, (TOK, TOK), 1)).astype(F32).astype(BF16)
    rank = jnp.dot(named.astype(BF16), earlier, preferred_element_type=F32)
    rank = jnp.where(named > 0.0, rank, -1.0)
    slot = lax.broadcasted_iota(jnp.int32, (SLOTS, EXPERTS), 0).astype(F32)
    owner = jnp.floor((slot + 0.5) * (1.0 / CAP))
    place = slot - CAP * owner
    expert = lax.broadcasted_iota(jnp.int32, (SLOTS, EXPERTS), 1).astype(F32)
    spread = jnp.where(owner == expert, 1.0, 0.0).astype(BF16)
    rank_rows = jnp.dot(spread, rank.astype(BF16), preferred_element_type=F32)
    send_ref[...] = jnp.where(rank_rows == place[:, :1], 1.0, 0.0).astype(BF16)
    slot_t = lax.broadcasted_iota(jnp.int32, (1, SLOTS), 1).astype(F32)
    place_t = slot_t - CAP * jnp.floor((slot_t + 0.5) * (1.0 / CAP))
    rank_t = jnp.transpose(rank).astype(BF16)
    taken = lax.dot_general(rank_t, spread, NT, preferred_element_type=F32) == place_t
    gate = jnp.transpose(gate)
    high = gate.astype(BF16)
    low = (gate - high.astype(F32)).astype(BF16)
    for part, ref in ((high, high_ref), (low, low_ref)):
        wide = lax.dot_general(part, spread, NT, preferred_element_type=F32)
        ref[...] = jnp.where(taken, wide, 0.0).astype(BF16)


def slot_matrices(where, ids, gates):
    whole = pl.BlockSpec(memory_space=pltpu.VMEM)
    return pl.pallas_call(
        slot_kernel,
        in_specs=[pl.BlockSpec(memory_space=pltpu.SMEM)] + [whole] * 2,
        out_specs=(whole,) * 3,
        out_shape=(
            jax.ShapeDtypeStruct((SLOTS, TOK), BF16),
            jax.ShapeDtypeStruct((TOK, SLOTS), BF16),
            jax.ShapeDtypeStruct((TOK, SLOTS), BF16),
        ),
        compiler_params=params(16),
        cost_estimate=pl.CostEstimate(flops=40_000_000, bytes_accessed=1_000_000, transcendentals=0),
        name="slots",
    )(where, ids, gates)


def attention_kernel(where_ref, q_ref, seg_ref, res_ref, gain_ref, send_ref, *rest):
    blocks = rest[:8]
    hidden_ref, out_ref, kv, segs, bias, hidden = rest[8:]
    x, zh, c = where_ref[0], where_ref[1], where_ref[2]
    for other_zh in (0, 1):
        for other_c in (0, 1):
            for back in (0, 1, 2):
                if other_c == 0:
                    block, top = blocks[other_zh * 3 + back], 0
                else:
                    block, top = blocks[6 + other_zh], back * PACK
                zh_at = zh if other_zh == 0 else 1 - zh
                c_at = c if other_c == 0 else 1 - c
                slot = (2 - back) * 4 + zh_at * 2 + c_at
                kv[pl.ds(pl.multiple_of(slot * TOK, TOK), TOK), :] = block[top : top + TOK, :]
                row = block[top + TOK : top + PACK, :TOK].astype(F32)
                segs[pl.ds(slot, 1), :] = row[:1, :]
    first = zh * 2 + c
    own = x * 4 + first
    t = lax.broadcasted_iota(jnp.int32, (TOK, TOK), 0)
    s = lax.broadcasted_iota(jnp.int32, (TOK, TOK), 1)
    mine = jnp.sum(jnp.where(s == t, seg_ref[...].astype(F32), 0.0), axis=1, keepdims=True)
    for i in range(WINDOW):
        number = own - (WINDOW - 1) + i
        same = segs[pl.ds(first + i, 1), :] == mine
        allowed = same & (number >= 0)
        if i == WINDOW - 1:
            allowed = allowed & (s <= t)
        bias[:, i * TOK : (i + 1) * TOK] = jnp.where(allowed, 0.0, -1e30)
    start = pl.multiple_of(first * TOK, TOK)
    rate = HD ** (-0.5) * 1.4426950408889634
    for g in range(KVH):
        key = kv[pl.ds(start, WINDOW * TOK), g * HD : (g + 1) * HD]
        value = kv[pl.ds(start, WINDOW * TOK), (KVH + g) * HD : (KVH + g + 1) * HD]
        for j in range(GROUPS):
            columns = slice((g * GROUPS + j) * HD, (g * GROUPS + j + 1) * HD)
            score = lax.dot_general(q_ref[:, columns], key, NT, preferred_element_type=F32)
            score = score + bias[...]
            peak = jnp.max(score, axis=-1, keepdims=True)
            weight = jnp.exp2((score - peak) * rate)
            total = jnp.sum(weight, axis=-1, keepdims=True)
            mixed = jnp.dot(weight.astype(BF16), value, preferred_element_type=F32)
            hidden[:, columns] = res_ref[:, columns].astype(F32) + mixed / total
    full = hidden[...]
    hidden_ref[...] = full
    mean = jnp.mean(full * full, axis=-1, keepdims=True)
    normed = (full * lax.rsqrt(mean + 1e-6) * gain_ref[...].astype(F32)).astype(BF16)
    for n in range(0, D, 512):
        out_ref[:, n : n + 512] = jnp.dot(
            send_ref[...], normed[:, n : n + 512], preferred_element_type=F32
        ).astype(BF16)


def attention(where, q, seg, res, gain, send, blocks):
    whole = pl.BlockSpec(memory_space=pltpu.VMEM)
    return pl.pallas_call(
        attention_kernel,
        in_specs=[pl.BlockSpec(memory_space=pltpu.SMEM)] + [whole] * (5 + 8),
        out_specs=(whole, whole),
        out_shape=(
            jax.ShapeDtypeStruct((TOK, D), F32),
            jax.ShapeDtypeStruct((SLOTS, D), BF16),
        ),
        scratch_shapes=[
            pltpu.VMEM((BLOCKS * TOK, 2 * KVH * HD), BF16),
            pltpu.VMEM((16, TOK), F32),
            pltpu.VMEM((TOK, WINDOW * TOK), F32),
            pltpu.VMEM((TOK, D), F32),
        ],
        compiler_params=params(20),
        cost_estimate=pl.CostEstimate(
            flops=1_900_000_000, bytes_accessed=9_000_000, transcendentals=2_400_000
        ),
        name="attend",
    )(where, q, seg, res, gain, send, *blocks)


def slice_place(expert, x, zh, c):
    return (expert + 8 * zh + (x - 4 if c == 0 else 3 - x)) % 16


STEP = 576


def expert_kernel(where_ref, x_ref, w_hbm, out_ref, w_ref, down_ref, sem_w):
    x = where_ref[0]
    chunks = range(0, SLOTS, STEP)

    def source(which, k):
        place = slice_place(2 * x + which, k // 4, (k // 2) % 2, k % 2)
        return pl.ds(pl.multiple_of((which * 16 + place) * TOK, TOK), TOK)

    def weight_slice(which, k):
        return pltpu.make_async_copy(
            w_hbm.at[source(which, k)], w_ref.at[which, pl.ds(k * TOK, TOK)], sem_w.at[which, k]
        )

    def start(which, half):
        for k in range(half * 8, half * 8 + 8):
            weight_slice(which, k).start()

    def wait(which, half):
        for k in range(half * 8, half * 8 + 8):
            weight_slice(which, k).wait()

    start(0, 0)
    start(0, 1)

    def run(which, spans, first):
        def rows(columns):
            return jnp.concatenate([x_ref[a:b, columns] for a, b in spans], axis=0)

        gate_up = None
        if first:
            for half in (0, 1):
                wait(which, half)
                if which == 0:
                    start(1, half)
                for j in range(0, FF, TOK):
                    for k in range(half * 8, half * 8 + 8):
                        down_ref[which, j : j + TOK, k * TOK : (k + 1) * TOK] = w_ref[
                            which, k * TOK : (k + 1) * TOK, 2 * FF + j : 2 * FF + j + TOK
                        ]
                if which == 0:
                    part = slice(half * 1024, half * 1024 + 1024)
                    term = jnp.dot(
                        rows(part), w_ref[which, part, : 2 * FF], preferred_element_type=F32
                    )
                    gate_up = term if gate_up is None else gate_up + term
        if gate_up is None:
            gate_up = jnp.dot(
                rows(slice(0, D)), w_ref[which, :, : 2 * FF], preferred_element_type=F32
            )
        gate, up = gate_up[:, :FF], gate_up[:, FF:]
        near = 0.5 * gate
        inner = ((near + near * jnp.tanh(near)) * up).astype(BF16)
        return jnp.dot(inner, down_ref[which], preferred_element_type=F32).astype(BF16)

    line = lax.broadcasted_iota(jnp.int32, (16, 1), 0)
    for which in (0, 1):
        for i, chunk in enumerate(chunks):
            starts = range(chunk, chunk + STEP, 144)
            if which == 0:
                y = run(0, [(a + b, a + b + 48) for a in starts for b in (0, 96)], i == 0)
                for n, a in enumerate(starts):
                    out_ref[a : a + 48, :] = y[n * 96 : n * 96 + 48]
                    out_ref[a + 96 : a + 144, :] = y[n * 96 + 48 : n * 96 + 96]
            else:
                y = run(1, [(a + 32, a + 112) for a in starts], i == 0)
                for n, a in enumerate(starts):
                    p = y[n * 80 : n * 80 + 80]
                    head, tail = out_ref[a + 32 : a + 48, :], out_ref[a + 96 : a + 112, :]
                    out_ref[a + 32 : a + 48, :] = jnp.where(line < 4, head, p[:16])
                    out_ref[a + 48 : a + 96, :] = p[16:64]
                    out_ref[a + 96 : a + 112, :] = jnp.where(line < 12, p[64:], tail)


def experts(where, x, both):
    hbm = pl.BlockSpec(memory_space=pltpu.HBM)
    whole = pl.BlockSpec(memory_space=pltpu.VMEM)
    return pl.pallas_call(
        expert_kernel,
        in_specs=[pl.BlockSpec(memory_space=pltpu.SMEM), whole, hbm],
        out_specs=whole,
        out_shape=jax.ShapeDtypeStruct((SLOTS, D), BF16),
        scratch_shapes=[
            pltpu.VMEM((2, D, 3 * FF), BF16),
            pltpu.VMEM((2, FF, D), BF16),
            pltpu.SemaphoreType.DMA((2, 16)),
        ],
        compiler_params=params(44),
        cost_estimate=pl.CostEstimate(
            flops=6_600_000_000, bytes_accessed=19_000_000, transcendentals=540_000
        ),
        name="expert_mlp",
    )(where, x, both)


def combine_kernel(hidden_ref, high_ref, low_ref, back_ref, out_ref):
    back = back_ref[...]
    routed = jnp.dot(high_ref[...], back, preferred_element_type=F32)
    routed = routed + jnp.dot(low_ref[...], back, preferred_element_type=F32)
    out_ref[...] = (hidden_ref[...] + routed).astype(BF16)


def combine(hidden, high, low, back):
    wide = 512
    return pl.pallas_call(
        combine_kernel,
        grid=(D // wide,),
        in_specs=[
            pl.BlockSpec((TOK, wide), lambda i: (0, i)),
            pl.BlockSpec((TOK, SLOTS), lambda i: (0, 0)),
            pl.BlockSpec((TOK, SLOTS), lambda i: (0, 0)),
            pl.BlockSpec((SLOTS, wide), lambda i: (0, i)),
        ],
        out_specs=pl.BlockSpec((TOK, wide), lambda i: (0, i)),
        out_shape=jax.ShapeDtypeStruct((TOK, D), BF16),
        compiler_params=params(16),
        cost_estimate=pl.CostEstimate(
            flops=1_200_000_000, bytes_accessed=7_000_000, transcendentals=0
        ),
        name="combine",
    )(hidden, high, low, back)


def shifted(steps):
    return [(x, x + steps) for x in range(4 - steps)]


def to_expert_column():
    pairs = []
    for k in range(16):
        for zl in range(8):
            place = slice_place(zl, k // 4, (k // 2) % 2, k % 2)
            target = ((zl // 2 * 2 + place // 8) * 2 + zl % 2) * 8 + place % 8
            pairs.append((k * 8 + zl, target))
    return pairs


def body(q, k, v, seg, res, gain, ids, gates, w_gate, w_up, w_down):
    x, zh, c, y = (lax.axis_index(a) for a in ("x", "zh", "c", "y"))
    swap = [(0, 1), (1, 0)]

    packet, packed = pack(k[0], v[0], w_gate[0], w_up[0], w_down[0], seg)
    packed = lax.ppermute(packed, ("x", "zh", "c", "zl"), to_expert_column())

    def spread(source):
        return [source] + [lax.ppermute(source, "x", shifted(back)) for back in (1, 2)]

    def other_core(found):
        return lax.ppermute(jnp.concatenate(found, axis=0), "c", swap)

    packet_zh = lax.ppermute(packet, "zh", swap)
    near = spread(packet)
    packet_zh, near = lax.optimization_barrier((packet_zh, near))
    far = spread(packet_zh)
    where = jnp.stack([x, zh, c, y]).astype(jnp.int32)
    ready = (*slot_matrices(where, ids[0].T, gates[0].T), gain[None], seg)
    packed, far, ready = lax.optimization_barrier((packed, far, ready))
    both = lax.all_gather(packed, ("c", "zh", "zl"), axis=0, tiled=True)
    blocks = [*near, *far, other_core(near), other_core(far)]

    send, high, low, gain_row, seg_row = ready
    hidden, outgoing = attention(where, q[0], seg_row, res[0], gain_row, send, blocks)
    arrived = lax.all_to_all(outgoing, ("x", "y"), 0, 0, tiled=True)
    done = experts(where, arrived, both)
    back = lax.all_to_all(done, ("x", "y"), 0, 0, tiled=True)
    return combine(hidden, high, low, back)[None]


def solution(mesh):
    fine = Mesh(mesh.devices.reshape(4, 2, 2, 4, 8), AXES)
    exp, ctx = ("y", "zl"), ("x", "zh", "c")
    rows = P(exp, ctx, None)
    return jax.shard_map(
        body,
        mesh=fine,
        in_specs=(rows, rows, rows, P(exp, ctx), rows, P(), rows, rows, rows, rows, P(exp, None, ctx)),
        out_specs=rows,
        check_vma=False,
    )
```

```python
import functools

import jax
import jax.numpy as jnp
from jax import lax
from jax.experimental import pallas as pl
from jax.experimental.pallas import tpu as pltpu
from jax.sharding import Mesh, PartitionSpec as P

D = 2048
HEADS = 16
KVH = 2
GROUPS = HEADS // KVH
HD = 128
FF = 384
EXPERTS = 32
TOPK = 8
TOK = 128
CAP = 36
SLOTS = EXPERTS * CAP
PACK = 144
WINDOW = 9
BLOCKS = 12
AXES = ("x", "zh", "c", "y", "zl")
F32 = jnp.float32
BF16 = jnp.bfloat16
NT = (((1,), (1,)), ((), ()))


def params(mib):
    return pltpu.CompilerParams(vmem_limit_bytes=mib * 1024 * 1024)


def pack_kernel(k_in, v_in, gate_in, up_in, down_in, seg_ref, packet_ref, packed_ref, sem):
    pieces = [
        (gate_in, packed_ref.at[:, pl.ds(0, FF)]),
        (up_in, packed_ref.at[:, pl.ds(FF, FF)]),
        (k_in, packet_ref.at[pl.ds(0, TOK), pl.ds(0, KVH * HD)]),
        (v_in, packet_ref.at[pl.ds(0, TOK), pl.ds(KVH * HD, KVH * HD)]),
    ]
    for j in range(0, FF, TOK):
        pieces.append((down_in.at[pl.ds(j, TOK)], packed_ref.at[:, pl.ds(2 * FF + j, TOK)]))
    copies = [pltpu.make_async_copy(a, b, sem.at[n]) for n, (a, b) in enumerate(pieces)]
    for copy in copies:
        copy.start()
    line = lax.broadcasted_iota(jnp.int32, (PACK - TOK, TOK), 0)
    row = jnp.where(line == 0, seg_ref[...].astype(F32), 0.0)
    packet_ref[TOK:, :TOK] = row.astype(BF16)
    packet_ref[TOK:, TOK:] = jnp.zeros((PACK - TOK, 2 * KVH * HD - TOK), BF16)
    for copy in copies:
        copy.wait()


def pack(k, v, w_gate, w_up, w_down, seg):
    whole = pl.BlockSpec(memory_space=pltpu.VMEM)
    return pl.pallas_call(
        pack_kernel,
        in_specs=[pl.BlockSpec(memory_space=pl.ANY)] * 5 + [whole],
        out_specs=(whole, whole),
        out_shape=(
            jax.ShapeDtypeStruct((PACK, 2 * KVH * HD), BF16),
            jax.ShapeDtypeStruct((TOK, 3 * FF), BF16),
        ),
        scratch_shapes=[pltpu.SemaphoreType.DMA((4 + FF // TOK,))],
        compiler_params=params(56),
        cost_estimate=pl.CostEstimate(flops=0, bytes_accessed=1_000_000, transcendentals=0),
        name="pack",
    )(k, v, w_gate, w_up, w_down, seg)


def slot_kernel(where_ref, ids_ref, gates_ref, send_ref, high_ref, low_ref):
    e = ids_ref[...]
    half = (e & 1) ^ (where_ref[3] & 1)
    ids = ((e >> 1) & 3) * 8 + (e >> 3) * 2 + half
    gates = gates_ref[...]
    line = lax.broadcasted_iota(jnp.int32, (EXPERTS, TOK), 0)
    named = jnp.zeros((EXPERTS, TOK), F32)
    gate = jnp.zeros((EXPERTS, TOK), F32)
    for k in range(TOPK):
        hit = ids[k : k + 1, :] == line
        named = named + jnp.where(hit, 1.0, 0.0)
        gate = gate + jnp.where(hit, gates[k : k + 1, :], 0.0)
    row = lax.broadcasted_iota(jnp.int32, (TOK, TOK), 0)
    earlier = (row < lax.broadcasted_iota(jnp.int32, (TOK, TOK), 1)).astype(F32).astype(BF16)
    rank = jnp.dot(named.astype(BF16), earlier, preferred_element_type=F32)
    rank = jnp.where(named > 0.0, rank, -1.0)
    slot = lax.broadcasted_iota(jnp.int32, (SLOTS, EXPERTS), 0).astype(F32)
    owner = jnp.floor((slot + 0.5) * (1.0 / CAP))
    place = slot - CAP * owner
    expert = lax.broadcasted_iota(jnp.int32, (SLOTS, EXPERTS), 1).astype(F32)
    spread = jnp.where(owner == expert, 1.0, 0.0).astype(BF16)
    rank_rows = jnp.dot(spread, rank.astype(BF16), preferred_element_type=F32)
    send_ref[...] = jnp.where(rank_rows == place[:, :1], 1.0, 0.0).astype(BF16)
    slot_t = lax.broadcasted_iota(jnp.int32, (1, SLOTS), 1).astype(F32)
    place_t = slot_t - CAP * jnp.floor((slot_t + 0.5) * (1.0 / CAP))
    rank_t = jnp.transpose(rank).astype(BF16)
    taken = lax.dot_general(rank_t, spread, NT, preferred_element_type=F32) == place_t
    gate = jnp.transpose(gate)
    high = gate.astype(BF16)
    low = (gate - high.astype(F32)).astype(BF16)
    for part, ref in ((high, high_ref), (low, low_ref)):
        wide = lax.dot_general(part, spread, NT, preferred_element_type=F32)
        ref[...] = jnp.where(taken, wide, 0.0).astype(BF16)


def slot_matrices(where, ids, gates):
    whole = pl.BlockSpec(memory_space=pltpu.VMEM)
    return pl.pallas_call(
        slot_kernel,
        in_specs=[pl.BlockSpec(memory_space=pltpu.SMEM)] + [whole] * 2,
        out_specs=(whole,) * 3,
        out_shape=(
            jax.ShapeDtypeStruct((SLOTS, TOK), BF16),
            jax.ShapeDtypeStruct((TOK, SLOTS), BF16),
            jax.ShapeDtypeStruct((TOK, SLOTS), BF16),
        ),
        compiler_params=params(16),
        cost_estimate=pl.CostEstimate(flops=40_000_000, bytes_accessed=1_000_000, transcendentals=0),
        name="slots",
    )(where, ids, gates)


def attention_kernel(where_ref, q_ref, seg_ref, res_ref, gain_ref, send_ref, *rest):
    blocks = rest[:8]
    hidden_ref, out_ref, kv, segs, bias, hidden = rest[8:]
    x, zh, c = where_ref[0], where_ref[1], where_ref[2]
    for other_zh in (0, 1):
        for other_c in (0, 1):
            for back in (0, 1, 2):
                if other_c == 0:
                    block, top = blocks[other_zh * 3 + back], 0
                else:
                    block, top = blocks[6 + other_zh], back * PACK
                zh_at = zh if other_zh == 0 else 1 - zh
                c_at = c if other_c == 0 else 1 - c
                slot = (2 - back) * 4 + zh_at * 2 + c_at
                kv[pl.ds(pl.multiple_of(slot * TOK, TOK), TOK), :] = block[top : top + TOK, :]
                row = block[top + TOK : top + PACK, :TOK].astype(F32)
                segs[pl.ds(slot, 1), :] = row[:1, :]
    first = zh * 2 + c
    own = x * 4 + first
    t = lax.broadcasted_iota(jnp.int32, (TOK, TOK), 0)
    s = lax.broadcasted_iota(jnp.int32, (TOK, TOK), 1)
    mine = jnp.sum(jnp.where(s == t, seg_ref[...].astype(F32), 0.0), axis=1, keepdims=True)
    for i in range(WINDOW):
        number = own - (WINDOW - 1) + i
        same = segs[pl.ds(first + i, 1), :] == mine
        allowed = same & (number >= 0)
        if i == WINDOW - 1:
            allowed = allowed & (s <= t)
        bias[:, i * TOK : (i + 1) * TOK] = jnp.where(allowed, 0.0, -1e30)
    start = pl.multiple_of(first * TOK, TOK)
    rate = HD ** (-0.5) * 1.4426950408889634
    for g in range(KVH):
        key = kv[pl.ds(start, WINDOW * TOK), g * HD : (g + 1) * HD]
        value = kv[pl.ds(start, WINDOW * TOK), (KVH + g) * HD : (KVH + g + 1) * HD]
        for j in range(GROUPS):
            columns = slice((g * GROUPS + j) * HD, (g * GROUPS + j + 1) * HD)
            score = lax.dot_general(q_ref[:, columns], key, NT, preferred_element_type=F32)
            score = score + bias[...]
            peak = jnp.max(score, axis=-1, keepdims=True)
            weight = jnp.exp2((score - peak) * rate)
            total = jnp.sum(weight, axis=-1, keepdims=True)
            mixed = jnp.dot(weight.astype(BF16), value, preferred_element_type=F32)
            hidden[:, columns] = res_ref[:, columns].astype(F32) + mixed / total
    full = hidden[...]
    hidden_ref[...] = full
    mean = jnp.mean(full * full, axis=-1, keepdims=True)
    normed = (full * lax.rsqrt(mean + 1e-6) * gain_ref[...].astype(F32)).astype(BF16)
    for n in range(0, D, 512):
        out_ref[:, n : n + 512] = jnp.dot(
            send_ref[...], normed[:, n : n + 512], preferred_element_type=F32
        ).astype(BF16)


def attention(where, q, seg, res, gain, send, blocks):
    whole = pl.BlockSpec(memory_space=pltpu.VMEM)
    return pl.pallas_call(
        attention_kernel,
        in_specs=[pl.BlockSpec(memory_space=pltpu.SMEM)] + [whole] * (5 + 8),
        out_specs=(whole, whole),
        out_shape=(
            jax.ShapeDtypeStruct((TOK, D), F32),
            jax.ShapeDtypeStruct((SLOTS, D), BF16),
        ),
        scratch_shapes=[
            pltpu.VMEM((BLOCKS * TOK, 2 * KVH * HD), BF16),
            pltpu.VMEM((16, TOK), F32),
            pltpu.VMEM((TOK, WINDOW * TOK), F32),
            pltpu.VMEM((TOK, D), F32),
        ],
        compiler_params=params(20),
        cost_estimate=pl.CostEstimate(
            flops=1_900_000_000, bytes_accessed=9_000_000, transcendentals=2_400_000
        ),
        name="attend",
    )(where, q, seg, res, gain, send, *blocks)


def slice_place(expert, x, zh, c):
    return (expert + 8 * zh + (x - 4 if c == 0 else 3 - x)) % 16


STEP = 576


def expert_kernel(where_ref, x_ref, w_hbm, out_ref, w_ref, down_ref, sem_w):
    x = where_ref[0]
    chunks = range(0, SLOTS, STEP)

    def source(which, k):
        place = slice_place(2 * x + which, k // 4, (k // 2) % 2, k % 2)
        return pl.ds(pl.multiple_of((which * 16 + place) * TOK, TOK), TOK)

    def weight_slice(which, k):
        return pltpu.make_async_copy(
            w_hbm.at[source(which, k)], w_ref.at[which, pl.ds(k * TOK, TOK)], sem_w.at[which, k]
        )

    def start(which, half):
        for k in range(half * 8, half * 8 + 8):
            weight_slice(which, k).start()

    def wait(which, half):
        for k in range(half * 8, half * 8 + 8):
            weight_slice(which, k).wait()

    start(0, 0)
    start(0, 1)

    def run(which, spans, first):
        def rows(columns):
            return jnp.concatenate([x_ref[a:b, columns] for a, b in spans], axis=0)

        gate_up = None
        if first:
            for half in (0, 1):
                wait(which, half)
                if which == 0:
                    start(1, half)
                for j in range(0, FF, TOK):
                    for k in range(half * 8, half * 8 + 8):
                        down_ref[which, j : j + TOK, k * TOK : (k + 1) * TOK] = w_ref[
                            which, k * TOK : (k + 1) * TOK, 2 * FF + j : 2 * FF + j + TOK
                        ]
                if which == 0:
                    part = slice(half * 1024, half * 1024 + 1024)
                    term = jnp.dot(
                        rows(part), w_ref[which, part, : 2 * FF], preferred_element_type=F32
                    )
                    gate_up = term if gate_up is None else gate_up + term
        if gate_up is None:
            gate_up = jnp.dot(
                rows(slice(0, D)), w_ref[which, :, : 2 * FF], preferred_element_type=F32
            )
        gate, up = gate_up[:, :FF], gate_up[:, FF:]
        near = 0.5 * gate
        inner = ((near + near * jnp.tanh(near)) * up).astype(BF16)
        return jnp.dot(inner, down_ref[which], preferred_element_type=F32).astype(BF16)

    line = lax.broadcasted_iota(jnp.int32, (16, 1), 0)
    for which in (0, 1):
        for i, chunk in enumerate(chunks):
            starts = range(chunk, chunk + STEP, 144)
            if which == 0:
                y = run(0, [(a + b, a + b + 48) for a in starts for b in (0, 96)], i == 0)
                for n, a in enumerate(starts):
                    out_ref[a : a + 48, :] = y[n * 96 : n * 96 + 48]
                    out_ref[a + 96 : a + 144, :] = y[n * 96 + 48 : n * 96 + 96]
            else:
                y = run(1, [(a + 32, a + 112) for a in starts], i == 0)
                for n, a in enumerate(starts):
                    p = y[n * 80 : n * 80 + 80]
                    head, tail = out_ref[a + 32 : a + 48, :], out_ref[a + 96 : a + 112, :]
                    out_ref[a + 32 : a + 48, :] = jnp.where(line < 4, head, p[:16])
                    out_ref[a + 48 : a + 96, :] = p[16:64]
                    out_ref[a + 96 : a + 112, :] = jnp.where(line < 12, p[64:], tail)


def experts(where, x, both):
    hbm = pl.BlockSpec(memory_space=pltpu.HBM)
    whole = pl.BlockSpec(memory_space=pltpu.VMEM)
    return pl.pallas_call(
        expert_kernel,
        in_specs=[pl.BlockSpec(memory_space=pltpu.SMEM), whole, hbm],
        out_specs=whole,
        out_shape=jax.ShapeDtypeStruct((SLOTS, D), BF16),
        scratch_shapes=[
            pltpu.VMEM((2, D, 3 * FF), BF16),
            pltpu.VMEM((2, FF, D), BF16),
            pltpu.SemaphoreType.DMA((2, 16)),
        ],
        compiler_params=params(44),
        cost_estimate=pl.CostEstimate(
            flops=6_600_000_000, bytes_accessed=19_000_000, transcendentals=540_000
        ),
        name="expert_mlp",
    )(where, x, both)


def combine_kernel(hidden_ref, high_ref, low_ref, back_ref, out_ref):
    parts = jnp.concatenate([high_ref[...], low_ref[...]], axis=0)
    routed = jnp.dot(parts, back_ref[...], preferred_element_type=F32)
    out_ref[...] = (hidden_ref[...] + (routed[:TOK] + routed[TOK:])).astype(BF16)


def combine(hidden, high, low, back):
    wide = 512
    return pl.pallas_call(
        combine_kernel,
        grid=(D // wide,),
        in_specs=[
            pl.BlockSpec((TOK, wide), lambda i: (0, i)),
            pl.BlockSpec((TOK, SLOTS), lambda i: (0, 0)),
            pl.BlockSpec((TOK, SLOTS), lambda i: (0, 0)),
            pl.BlockSpec((SLOTS, wide), lambda i: (0, i)),
        ],
        out_specs=pl.BlockSpec((TOK, wide), lambda i: (0, i)),
        out_shape=jax.ShapeDtypeStruct((TOK, D), BF16),
        compiler_params=params(16),
        cost_estimate=pl.CostEstimate(
            flops=1_200_000_000, bytes_accessed=7_000_000, transcendentals=0
        ),
        name="combine",
    )(hidden, high, low, back)


def shifted(steps):
    return [(x, x + steps) for x in range(4 - steps)]


def to_expert_column():
    pairs = []
    for k in range(16):
        for zl in range(8):
            place = slice_place(zl, k // 4, (k // 2) % 2, k % 2)
            target = ((zl // 2 * 2 + place // 8) * 2 + zl % 2) * 8 + place % 8
            pairs.append((k * 8 + zl, target))
    return pairs


def body(q, k, v, seg, res, gain, ids, gates, w_gate, w_up, w_down):
    x, zh, c, y = (lax.axis_index(a) for a in ("x", "zh", "c", "y"))
    swap = [(0, 1), (1, 0)]

    packet, packed = pack(k[0], v[0], w_gate[0], w_up[0], w_down[0], seg)
    packed = lax.ppermute(packed, ("x", "zh", "c", "zl"), to_expert_column())

    def spread(source):
        return [source] + [lax.ppermute(source, "x", shifted(back)) for back in (1, 2)]

    def other_core(found):
        return lax.ppermute(jnp.concatenate(found, axis=0), "c", swap)

    packet_zh = lax.ppermute(packet, "zh", swap)
    near = spread(packet)
    packet_zh, near = lax.optimization_barrier((packet_zh, near))
    far = spread(packet_zh)
    where = jnp.stack([x, zh, c, y]).astype(jnp.int32)
    ready = (*slot_matrices(where, ids[0].T, gates[0].T), gain[None], seg)
    packed, far, ready = lax.optimization_barrier((packed, far, ready))
    both = lax.all_gather(packed, ("c", "zh", "zl"), axis=0, tiled=True)
    blocks = [*near, *far, other_core(near), other_core(far)]

    send, high, low, gain_row, seg_row = ready
    hidden, outgoing = attention(where, q[0], seg_row, res[0], gain_row, send, blocks)
    arrived = lax.all_to_all(outgoing, ("x", "y"), 0, 0, tiled=True)
    done = experts(where, arrived, both)
    back = lax.all_to_all(done, ("x", "y"), 0, 0, tiled=True)
    return combine(hidden, high, low, back)[None]


def solution(mesh):
    fine = Mesh(mesh.devices.reshape(4, 2, 2, 4, 8), AXES)
    exp, ctx = ("y", "zl"), ("x", "zh", "c")
    rows = P(exp, ctx, None)
    return jax.shard_map(
        body,
        mesh=fine,
        in_specs=(rows, rows, rows, P(exp, ctx), rows, P(), rows, rows, rows, rows, P(exp, None, ctx)),
        out_specs=rows,
        check_vma=False,
    )
```
